256 devices in a mesh: mp: 16 (over y, z_hi), tp: 16 (over z_lo, x, core).
Axes of the slice: x: 4, y: 4, z: 8 (z_hi: 4, z_lo: 2; z = z_hi * 2 + z_lo), core: 2. Of those that a mesh axis runs over, the one named last changes fastest.
Arguments:
- activations: bfloat16 [16, 4, 256, 8192], P('mp', None, None, 'tp'), may hold values from -100 to 100
- cotangents: bfloat16 [16, 4, 256, 4096], P('mp', None, None, 'tp'), may hold values from -0.3984375 to 0.3984375
- checkpoints: bfloat16 [16, 8192, 4096], P('mp', 'tp'), may hold values from -6 to 6
Outputs:
- merged: bfloat16 [8192, 4096], P('tp')
The draws below stay inside these ranges and needn't reach their ends.
All inputs are finite; a program needn't handle non-finite values.
Results may differ from the reference program's by a relative error of at most 0.022.
Values may be sent and summed in bfloat16 or wider, within the bound.
No kernel may reach another device: no remote copies, remote signals or barrier semaphores. Data moves between devices by JAX's collectives and lax.ppermute only.
A program may use at most 128 MiB of HBM per device.

```python
import math
import jax
import jax.numpy as jnp
from jax import lax

D = 8192
TOK = 256
BATCHES = 4
COLS = 4096
MODELS = 16


def draw_activations(key, part):
    first, second = jax.random.split(key)
    base = jnp.clip(jax.random.normal(first, (MODELS, BATCHES, TOK, D), jnp.float32), -6.0, 6.0)
    scales = jnp.exp(jax.random.uniform(second, (MODELS, 1, 1, D), jnp.float32, 0.0, math.log(10.0)))
    return (base * scales).astype(jnp.bfloat16)


def spiked(values, stream_key, source, target, shards_of, factor):
    def block_of(dim):
        return (jnp.arange(values.shape[dim]) // (values.shape[dim] // shards_of)).reshape((-1,) + (1,) * (values.ndim - 1 - dim))

    first = jax.random.permutation(stream_key, shards_of)[block_of(target)]
    second = (block_of(target) + shards_of // 2) % shards_of
    return jnp.where((block_of(source) == first) | (block_of(source) == second), factor * values, values)


def levels(rng, shape, cuts, least, top_value):
    gain, own = 1.0, jax.random.fold_in(rng, 6)
    for dim, parts in cuts:
        heights = jnp.exp(jax.random.uniform(jax.random.fold_in(own, dim), (parts,), jnp.float32, least / len(cuts), top_value / len(cuts)))
        gain = gain * jnp.repeat(heights, shape[dim] // parts).reshape([-1 if axis == dim else 1 for axis in range(len(shape))])
    return gain


def normal_values(rng, dims, deviation, limit, pieces=(), held_as=jnp.bfloat16):
    values = deviation * jax.random.normal(rng, dims, jnp.float32)
    if pieces:
        values = values * levels(rng, dims, pieces, -0.22, 0.18)
    return jnp.clip(values, -limit, limit).astype(held_as)


def noise_with(key, extent, deviation, limit, cuts, heavy, kind=jnp.bfloat16):
    result = deviation * jax.random.normal(key, extent, jnp.float32)
    if cuts:
        result = result * levels(key, extent, cuts, -0.22, 0.18)
    return jnp.clip(spiked(result, jax.random.fold_in(key, 3), *heavy), -limit, limit).astype(kind)


def setup_inputs(seed: int = 0) -> dict:
    seeds = jax.random.split(jax.random.key(seed), 4)
    activations = draw_activations(jax.random.fold_in(seeds[3], 71), 0)
    cotangents = normal_values(seeds[1], (MODELS, BATCHES, TOK, COLS), 0.0625, 0.3984375, ((0, 16), (3, 16)))
    checkpoints = noise_with(seeds[2], (MODELS, D, COLS), 1.0, 6.0, ((0, 16), (1, 16)), (0, 1, 16, 2.0))
    return dict(activations=activations, cotangents=cotangents, checkpoints=checkpoints)


def reference(activations, cotangents, checkpoints):
    def one_model(carry, index):
        numer, denom = carry
        fisher = jnp.zeros((D, COLS), jnp.float32)
        for number in range(BATCHES):
            inputs = lax.dynamic_index_in_dim(activations, index, 0, keepdims=False)[number]
            grads_out = lax.dynamic_index_in_dim(cotangents, index, 0, keepdims=False)[number]
            grad = jnp.dot(inputs.T, grads_out, preferred_element_type=jnp.float32)
            fisher = fisher + grad * grad
        weights = lax.dynamic_index_in_dim(checkpoints, index, 0, keepdims=False).astype(jnp.float32)
        weighted = lax.optimization_barrier((fisher * weights).astype(jnp.bfloat16))
        fisher_wire = lax.optimization_barrier(fisher.astype(jnp.bfloat16))
        return (numer + weighted.astype(jnp.float32), denom + fisher_wire.astype(jnp.float32)), None

    start = (jnp.zeros((D, COLS), jnp.float32), jnp.zeros((D, COLS), jnp.float32))
    (numer, denom), _ = lax.scan(one_model, start, jnp.arange(MODELS, dtype=jnp.int32))
    return (numer / denom).astype(jnp.bfloat16)
```

```python
import functools

import jax
import jax.numpy as jnp
from jax import lax
from jax.experimental import pallas as pl
from jax.experimental.pallas import tpu as pltpu
from jax.sharding import Mesh
from jax.sharding import PartitionSpec as P

BF = jnp.bfloat16
F32 = jnp.float32
TILE = 256
ROWS = 512
Q = 128
H = 64
S = 32
VMEM = 40 * 1024 * 1024


def shift(value, axis, step):
    n = lax.axis_size(axis)
    return lax.ppermute(value, axis, [(i, (i + step) % n) for i in range(n)])


def params():
    return pltpu.CompilerParams(vmem_limit_bytes=VMEM)


def fisher_kernel(where, acts, mine, peer, ck_mine, ck_peer, own, p1, p2, m1, m2, total):
    y = where[0]

    def rows(step, start, size):
        at = lax.rem(y + step, 4) * Q + start
        return pl.ds(pl.multiple_of(at, size), size)

    for side, (cots, weights) in enumerate(((mine, ck_mine), (peer, ck_peer))):
        for number in range(4):
            grad = jnp.dot(acts[number], cots[0, number], preferred_element_type=F32)
            if number == 0:
                total[...] = grad * grad
            else:
                total[...] += grad * grad
        cols = slice(side * TILE, (side + 1) * TILE)

        def put(ref, at, step, start, size):
            part = rows(step, start, size)
            value = total[part, :]
            out = slice(at, at + size)
            ref[0, out, cols] = (value * weights[part, :].astype(F32)).astype(BF)
            ref[1, out, cols] = value.astype(BF)

        put(own, 0, 0, 0, Q)
        put(p1, 0, 2, 0, H)
        put(p1, H, 1, H, H)
        put(p2, 0, 1, 0, H)
        put(m1, 0, 2, H, H)
        put(m1, H, 3, 0, H)
        put(m2, 0, 3, H, H)


def fisher_parts(acts, mine, peer, weights, where):
    chips = mine.shape[0]
    columns = 2 * TILE * chips
    cots = pl.BlockSpec((1, 4, 256, TILE), lambda i, s: (i, 0, 0, 0))

    def out(rows):
        return pl.BlockSpec((2, rows, 2 * TILE), lambda i, s: (0, 0, i))

    heights = (Q, Q, H, Q, H)
    return pl.pallas_call(
        fisher_kernel,
        out_shape=[jax.ShapeDtypeStruct((2, rows, columns), BF) for rows in heights],
        grid_spec=pltpu.PrefetchScalarGridSpec(
            num_scalar_prefetch=1,
            grid=(chips,),
            in_specs=[
                pl.BlockSpec((4, ROWS, 256), lambda i, s: (0, 0, 0)),
                cots,
                cots,
                pl.BlockSpec((ROWS, TILE), lambda i, s: (0, s[2 + 2 * i])),
                pl.BlockSpec((ROWS, TILE), lambda i, s: (0, s[3 + 2 * i])),
            ],
            out_specs=[out(rows) for rows in heights],
            scratch_shapes=[pltpu.VMEM((ROWS, TILE), F32)],
        ),
        compiler_params=params(),
        cost_estimate=pl.CostEstimate(
            flops=2 * ROWS * 1024 * columns, bytes_accessed=ROWS * columns * 10, transcendentals=0
        ),
        name="fisher_parts",
    )(where, acts, mine, peer, weights, weights)


def add_kernel(a, b, c, d, e, f):
    e[...] = (a[...].astype(F32) + b[...][:, :H].astype(F32)).astype(BF)
    f[...] = (c[...].astype(F32) + d[...][:, :H].astype(F32)).astype(BF)


def add_pair(p2, p1r, m2, m1r):
    shape = jax.ShapeDtypeStruct(p2.shape, BF)
    return pl.pallas_call(
        add_kernel, out_shape=[shape, shape], compiler_params=params(), name="add_pair"
    )(p2, p1r, m2, m1r)


def sum_kernel(where, own, p1r, m1r, p2r, m2r, o0, o1, o2, o3, total):
    w = where[1]
    total[:, :H] = own[:, :H].astype(F32) + p2r[...].astype(F32) + m1r[:, H:].astype(F32)
    total[:, H:] = own[:, H:].astype(F32) + p1r[:, H:].astype(F32) + m2r[...].astype(F32)
    for step, out in enumerate((o0, o1, o2, o3)):
        at = pl.multiple_of(lax.rem(w + step, 4) * S, S)
        out[...] = total[:, pl.ds(at, S), :].astype(out.dtype)


def sum_parts(own, p1r, m1r, p2r, m2r, where):
    columns = own.shape[2]
    whole = pl.BlockSpec((2, S, columns), lambda i, s: (0, 0, 0))

    def block(rows):
        return pl.BlockSpec((2, rows, columns), lambda i, s: (0, 0, 0))

    return pl.pallas_call(
        sum_kernel,
        out_shape=[jax.ShapeDtypeStruct((2, S, columns), t) for t in (F32, BF, BF, BF)],
        grid_spec=pltpu.PrefetchScalarGridSpec(
            num_scalar_prefetch=1,
            grid=(1,),
            in_specs=[block(Q), block(Q), block(Q), block(H), block(H)],
            out_specs=[whole] * 4,
            scratch_shapes=[pltpu.VMEM((2, Q, columns), F32)],
        ),
        compiler_params=params(),
        name="sum_parts",
    )(where, own, p1r, m1r, p2r, m2r)


def merge_kernel(own, a, b, c, out):
    total = own[...] + a[...].astype(F32) + b[...].astype(F32) + c[...].astype(F32)
    out[...] = (total[0] / total[1]).astype(BF)


def merge(own, a, b, c):
    return pl.pallas_call(
        merge_kernel,
        out_shape=jax.ShapeDtypeStruct(own.shape[1:], BF),
        compiler_params=params(),
        name="merge",
    )(own, a, b, c)


def place_kernel(first, where, z0, zm, zp, z2a, z2b, *refs):
    out = refs[-1]
    y, w = where[0], where[1]
    owners = (0, 3, 1, 2)

    def put(ref, at, step, part):
        row = lax.rem(y + step, 4) * Q + lax.rem(w + owners[part], 4) * S
        out[pl.ds(pl.multiple_of(row, S), S), :] = ref[at : at + S, :]

    for part in range(4):
        put(z0, part * S, 0, part)
        put(zm, part * S, 3, part)
        put(zp, part * S, 1, part)
    for part in range(2):
        put(z2a, part * S, 2, part)
        put(z2b, part * S, 2, part + 2)


def place(out, z0, zm, zp, z2a, z2b, where, total):
    columns = z0.shape[1]

    def block(rows):
        return pl.BlockSpec((rows, TILE), lambda i, s: (0, i))

    first = out is None
    return pl.pallas_call(
        functools.partial(place_kernel, first),
        out_shape=jax.ShapeDtypeStruct((ROWS, total), BF),
        grid_spec=pltpu.PrefetchScalarGridSpec(
            num_scalar_prefetch=1,
            grid=(columns // TILE,),
            in_specs=[block(Q), block(Q), block(Q), block(H), block(H)]
            + ([] if first else [pl.BlockSpec(memory_space=pl.ANY)]),
            out_specs=pl.BlockSpec((ROWS, TILE), lambda i, s: (0, s[2 + i])),
        ),
        input_output_aliases={} if first else {6: 0},
        compiler_params=params(),
        name="place",
    )(where, z0, zm, zp, z2a, z2b, *([] if first else [out]))


def on_device(activations, cotangents, checkpoints):
    y, w, v, x, c = (lax.axis_index(axis) for axis in ("y", "w", "v", "x", "c"))
    acts = jnp.swapaxes(activations[0], 1, 2)
    weights = checkpoints[0]
    own = cotangents[0]
    pair = jnp.stack([own, shift(own, "v", 1)])
    chunks = [(pair, 0)] + [(shift(pair, "x", step), step) for step in (1, -1, 2)]

    out = None
    for mine, step in chunks:
        peer = shift(mine, "c", 1)
        from_x = (x - step) % 4
        chips = [v * 4 + from_x, (1 - v) * 4 + from_x]
        where = [y, w]
        for chip in chips:
            where += [chip * 2 + c, chip * 2 + 1 - c]
        where = jnp.stack(where).astype(jnp.int32)
        mine0, p1, p2, m1, m2 = fisher_parts(acts, mine, peer, weights, where)
        p1r = shift(p1, "y", 1)
        m1r = shift(m1, "y", -1)
        p2, m2 = add_pair(p2, p1r, m2, m1r)
        p2r = shift(p2, "y", 1)
        m2r = shift(m2, "y", -1)
        o0, o1, o2, o3 = sum_parts(mine0, p1r, m1r, p2r, m2r, where)
        z = merge(o0, shift(o1, "w", 1), shift(o2, "w", 2), shift(o3, "w", -1))
        z0 = jnp.concatenate([z, shift(z, "w", 1), shift(z, "w", -1), shift(z, "w", 2)], axis=0)
        zm = shift(z0, "y", 1)
        zp = shift(z0, "y", -1)
        z2a = shift(zm[:H], "y", 1)
        z2b = shift(zp[H:], "y", -1)
        out = place(out, z0, zm, zp, z2a, z2b, where, weights.shape[1])
    return out


def solution(mesh):
    fine = Mesh(mesh.devices.reshape(4, 4, 2, 4, 2), ("y", "w", "v", "x", "c"))
    mp, tp = ("y", "w"), ("v", "x", "c")
    in_specs = (P(mp, None, None, tp), P(mp, None, None, tp), P(mp, tp, None))
    return jax.shard_map(
        on_device, mesh=fine, in_specs=in_specs, out_specs=P(tp, None), check_vma=False
    )
```

```python
import functools

import jax
import jax.numpy as jnp
from jax import lax
from jax.experimental import pallas as pl
from jax.experimental.pallas import tpu as pltpu
from jax.sharding import Mesh
from jax.sharding import PartitionSpec as P

BF = jnp.bfloat16
F32 = jnp.float32
TILE = 256
ROWS = 512
S = 32
MIB = 1024 * 1024
ORDER = (
    "hV SA SC A0",
    "hB C0 hD A1",
    "B0 D0 A2 C1",
    "A3 B1 A4 C2",
    "D1 C3 A5 A6",
    "B2 D2 B3 D3",
    "C4 B4 D4 C5",
    "B5 D5 D6 C6",
    "A7 D7 B6 A8",
    "C7 B7 D8 C8",
    "B8",
)
ORDER = [step for line in ORDER for step in line.split()]
GROUPS = ()
MERGE = 9
ANY = pl.BlockSpec(memory_space=pl.ANY)


def partner(i, core, which):
    swap = core if which == 0 else 1 - core
    return (i ^ 1) * (1 - swap) + (3 - i) * swap


def exchange(value, axis, which):
    pairs = [
        (i * 2 + core, partner(i, core, which) * 2 + core) for i in range(4) for core in range(2)
    ]
    return lax.ppermute(value, (axis, "c"), pairs)


def swap(value, axis):
    return lax.ppermute(value, axis, [(0, 1), (1, 0)])


def bits(i, core):
    flips = (i // 2 + i) % 2, i // 2
    return (
        flips[0] * (1 - core) + flips[1] * core,
        flips[1] * (1 - core) + flips[0] * core,
    )


def params(limit=8):
    return dict(
        compiler_params=pltpu.CompilerParams(vmem_limit_bytes=limit * MIB),
        cost_estimate=pl.CostEstimate(flops=1, bytes_accessed=1, transcendentals=0),
    )


def hold_kernel(value, after, out):
    pass


def hold(value, after):
    return pl.pallas_call(
        hold_kernel,
        out_shape=jax.ShapeDtypeStruct(value.shape, value.dtype),
        in_specs=[ANY, ANY],
        out_specs=ANY,
        input_output_aliases={0: 0},
        name="hold",
        **params(),
    )(value, after)


def stack_kernel(a, b, after, out):
    out[0] = a[...]
    out[1] = b[...]


def stack(a, b, after):
    whole = pl.BlockSpec(memory_space=pltpu.VMEM)
    return pl.pallas_call(
        stack_kernel,
        out_shape=jax.ShapeDtypeStruct((2, *a.shape), BF),
        in_specs=[whole, whole, ANY],
        out_specs=whole,
        name="stack",
        **params(),
    )(a, b, after)


def fisher_kernel(where, acts, mine, peer, weights, after, send, keep, total, tiles, sems):
    mark = where[0]
    chips = mine.shape[0]

    def fetch(tile):
        column = pl.multiple_of(where[1 + tile] * TILE, TILE)
        return pltpu.make_async_copy(
            weights.at[:, pl.ds(column, TILE)], tiles.at[tile], sems.at[tile]
        )

    for tile in range(2 * chips):
        fetch(tile).start()
    for tile in range(2 * chips):
        cots = (mine, peer)[tile % 2]
        for number in range(4):
            grad = jnp.dot(acts[number], cots[tile // 2, number], preferred_element_type=F32)
            if number == 0:
                total[...] = grad * grad
            else:
                total[...] += grad * grad
        fetch(tile).wait()
        cols = slice(tile * TILE, (tile + 1) * TILE)
        for k in range(16):
            part = pl.ds(pl.multiple_of((mark ^ (15 - k)) * S, S), S)
            value = total[part, :]
            ref, at = (send, k) if k < 8 else (keep, k - 8)
            out = slice(at * S, (at + 1) * S)
            ref[0, out, cols] = (value * tiles[tile, part, :].astype(F32)).astype(BF)
            ref[1, out, cols] = value.astype(BF)


def fisher_parts(acts, mine, peer, weights, where, after):
    chips = mine.shape[0]
    columns = 2 * TILE * chips
    whole = pl.BlockSpec(memory_space=pltpu.VMEM)
    return pl.pallas_call(
        fisher_kernel,
        out_shape=[jax.ShapeDtypeStruct((2, ROWS // 2, columns), BF)] * 2,
        in_specs=[
            pl.BlockSpec(memory_space=pltpu.SMEM),
            whole,
            whole,
            whole,
            pl.BlockSpec(memory_space=pltpu.HBM),
            ANY,
        ],
        out_specs=[whole, whole],
        scratch_shapes=[
            pltpu.VMEM((ROWS, TILE), F32),
            pltpu.VMEM((2 * chips, ROWS, TILE), BF),
            pltpu.SemaphoreType.DMA((2 * chips,)),
        ],
        name="fisher_parts",
        **params(14),
    )(where, acts, mine, peer, weights, after)


def add_kernel(split, divide, *refs):
    out, refs = refs[-1], refs[:-2]
    counts, columns = split
    at = 0
    parts = []
    for count, width in zip(counts, columns):
        parts.append(refs[at : at + count])
        at += count
    joint = refs[at:]
    first = 0
    for own, width in zip(parts, columns):
        cols = slice(first, first + width)
        first += width
        total = own[0][...].astype(F32)
        for ref in own[1:]:
            total = total + ref[...].astype(F32)
        for ref in joint:
            total = total + ref[:, :, cols].astype(F32)
        if divide:
            out[:, cols] = (total[0] / total[1]).astype(BF)
        else:
            out[:, :, cols] = total.astype(BF)


def add_up(parts, joint, rows, after, divide):
    widths = tuple(part[0][0].shape[2] for part in parts)
    columns = sum(widths)
    shape = (rows, columns) if divide else (2, rows, columns)
    arrays = [pair for part in parts for pair in part] + joint

    def block(array, at):
        return pl.BlockSpec((2, rows, array.shape[2]), lambda i: (0, at // rows, 0))

    split = tuple(len(part) for part in parts), widths
    return pl.pallas_call(
        functools.partial(add_kernel, split, divide),
        out_shape=jax.ShapeDtypeStruct(shape, BF),
        grid=(1,),
        in_specs=[block(*pair) for pair in arrays] + [ANY],
        out_specs=pl.BlockSpec(shape, lambda i: (0,) * len(shape)),
        name="merge" if divide else "add_up",
        **params(),
    )(*[array for array, _ in arrays], after)


def join_kernel(a, b, after, out):
    rows = a.shape[0]
    out[:rows] = a[...]
    out[rows:] = b[...]


def join(a, b, after):
    whole = pl.BlockSpec(memory_space=pltpu.VMEM)
    return pl.pallas_call(
        join_kernel,
        out_shape=jax.ShapeDtypeStruct((2 * a.shape[0], a.shape[1]), BF),
        in_specs=[whole, whole, ANY],
        out_specs=whole,
        name="join",
        **params(),
    )(a, b, after)


def place_kernel(where, far, near, *refs):
    out = refs[-1]
    mark = where[0]
    for k in range(16):
        ref, at = (far, k) if k < 8 else (near, k - 8)
        part = pl.ds(pl.multiple_of((mark ^ (15 - k)) * S, S), S)
        out[part, :] = ref[at * S : (at + 1) * S, :]


def place(out, far, near, at, chips, where, weights, after):
    tiles = 2 * chips
    block = pl.BlockSpec((ROWS // 2, TILE), lambda i, s: (0, i + 2 * at))
    extra = [after] if out is None else [after, out]
    return pl.pallas_call(
        place_kernel,
        out_shape=jax.ShapeDtypeStruct(weights.shape, BF),
        grid_spec=pltpu.PrefetchScalarGridSpec(
            num_scalar_prefetch=1,
            grid=(tiles,),
            in_specs=[block, block] + [ANY] * len(extra),
            out_specs=pl.BlockSpec((ROWS, TILE), lambda i, s: (0, s[1 + i])),
        ),
        input_output_aliases={} if out is None else {4: 0},
        name="place",
        **params(),
    )(where, far, near, *extra)


def on_device(activations, cotangents, checkpoints):
    y, w, v, x, c = (lax.axis_index(axis) for axis in ("y", "w", "v", "x", "c"))
    weights = checkpoints[0]
    own = cotangents[0]
    y1, y2 = bits(y, c)
    w1, w2 = bits(w, c)
    mark = y1 * 8 + w1 * 4 + y2 * 2 + w2

    near = exchange(own, "x", 0)
    other = swap(own, "v")
    acts = jnp.swapaxes(activations[0], 1, 2)

    def chip(which, core):
        first = partner(x, core, 0)
        second = partner(x, core, 1)
        return (x, first, second, partner(second, core, 0))[which]

    def places(layer, pair):
        tiles = [mark]
        for which in pair:
            for core in (c, 1 - c):
                tiles.append((layer * 4 + chip(which, core)) * 2 + core)
        return jnp.stack(tiles).astype(jnp.int32)

    where = {
        "A": places(v, (0, 1)),
        "B": places(v, (2, 3)),
        "C": places(1 - v, (0, 1)),
        "D": places(1 - v, (2, 3)),
    }
    mine, peer = {}, {}
    parts = {name: [] for name in where}
    joint = {group: [] for group in GROUPS}
    made = {}
    last, out = acts, None

    for step in ORDER:
        if step == "SA":
            last = mine["A"] = stack(own, near, last)
            peer["A"] = swap(mine["A"], "c")
            mine["B"] = exchange(mine["A"], "x", 1)
            continue
        if step == "hV":
            last = other = hold(other, last)
            beyond = exchange(other, "x", 0)
            continue
        if step == "SC":
            last = mine["C"] = stack(other, beyond, last)
            peer["C"] = swap(mine["C"], "c")
            mine["D"] = exchange(mine["C"], "x", 1)
            continue
        if step in ("hB", "hD"):
            name = step[1]
            last = mine[name] = hold(mine[name], last)
            peer[name] = swap(mine[name], "c")
            continue
        name, stage = step[:-1], int(step[-1])
        have = made.get(name)
        axis = "yw"[(stage if stage < 4 else 7 - stage) % 2]
        which = (stage if stage < 4 else 7 - stage) // 2
        if stage == 0:
            send, keep = fisher_parts(acts, mine[name], peer[name], weights, where[name], last)
            parts[name] = [(keep, 0), (exchange(send, axis, which), 0)]
            last = send
        elif stage < 5:
            rows = (128, 64, 32, 32)[stage - 1]
            start = (0, 128, 192, 224)[stage - 1]
            chunks = [[(a, start - f) for a, f in parts[c]] for c in name]
            both = [(a, start - f) for a, f in joint.get(name, [])]
            last = add_up(chunks, both, rows, last, stage == 4)
            if stage < 4:
                came = exchange(last, axis, which), start + rows
                (joint[name] if name in joint and stage >= MERGE else parts[name]).append(came)
            else:
                made[name] = [last, exchange(last, axis, which)]
        elif stage < 8:
            last = join(have[1], have[0], last)
            made[name] = [last, exchange(last, axis, which)]
        else:
            at = 0
            for c in name:
                out = place(out, have[1], have[0], at, mine[c].shape[0], where[c], weights, last)
                at += mine[c].shape[0]
    return out


def solution(mesh):
    fine = Mesh(mesh.devices.reshape(4, 4, 2, 4, 2), ("y", "w", "v", "x", "c"))
    mp, tp = ("y", "w"), ("v", "x", "c")
    in_specs = (P(mp, None, None, tp), P(mp, None, None, tp), P(mp, tp, None))
    return jax.shard_map(
        on_device, mesh=fine, in_specs=in_specs, out_specs=P(tp, None), check_vma=False
    )
```

```python
import functools

import jax
import jax.numpy as jnp
from jax import lax
from jax.experimental import pallas as pl
from jax.experimental.pallas import tpu as pltpu
from jax.sharding import Mesh
from jax.sharding import PartitionSpec as P

BF = jnp.bfloat16
F32 = jnp.float32
TILE = 256
ROWS = 512
S = 32
MIB = 1024 * 1024
ORDER = (
    "SA A0 hB hV",
    "SC A1 B0 A2",
    "hD C0 B1 A3",
    "D0 B2 A4 B3",
    "C1 D1 C2 B4",
    "A5 D2 C3 A6",
    "D3 B5 C4 A7",
    "B6 D4 C5 D5",
    "C6 B7 D6 C7",
    "D7",
)
ORDER = [step for line in ORDER for step in line.split()]
EXCHANGES = (
    ("y", 0),
    ("y", 1),
    ("w", 0),
    ("w", 1),
    ("w", 0),
    ("y", 1),
    ("y", 0),
)
ANY = pl.BlockSpec(memory_space=pl.ANY)
TOKEN = jax.ShapeDtypeStruct((8, 128), F32)


def partner(i, core, which):
    swap = core if which == 0 else 1 - core
    return (i ^ 1) * (1 - swap) + (3 - i) * swap


def exchange(value, axis, which):
    pairs = [
        (i * 2 + core, partner(i, core, which) * 2 + core) for i in range(4) for core in range(2)
    ]
    return lax.ppermute(value, (axis, "c"), pairs)


def swap(value, axis):
    return lax.ppermute(value, axis, [(0, 1), (1, 0)])


def bits(i, core):
    flips = (i // 2 + i) % 2, i // 2
    return (
        flips[0] * (1 - core) + flips[1] * core,
        flips[1] * (1 - core) + flips[0] * core,
    )


def params(limit=8):
    return dict(
        compiler_params=pltpu.CompilerParams(vmem_limit_bytes=limit * MIB),
        cost_estimate=pl.CostEstimate(flops=1, bytes_accessed=1, transcendentals=0),
    )


def hold_kernel(value, after, out, token):
    pass


def hold(value, after):
    return pl.pallas_call(
        hold_kernel,
        out_shape=[jax.ShapeDtypeStruct(value.shape, value.dtype), TOKEN],
        in_specs=[ANY, ANY],
        out_specs=[ANY, ANY],
        input_output_aliases={0: 0},
        name="hold",
        **params(),
    )(value, after)


def stack_kernel(a, b, after, out, token):
    out[0] = a[...]
    out[1] = b[...]


def stack(a, b, after):
    whole = pl.BlockSpec(memory_space=pltpu.VMEM)
    return pl.pallas_call(
        stack_kernel,
        out_shape=[jax.ShapeDtypeStruct((2, *a.shape), BF), TOKEN],
        in_specs=[whole, whole, ANY],
        out_specs=[whole, ANY],
        name="stack",
        **params(),
    )(a, b, after)


def fisher_kernel(where, acts, mine, peer, weights, after, send, keep, token, total, tiles, sems):
    mark = where[0]
    chips = mine.shape[0]

    def fetch(tile):
        column = pl.multiple_of(where[1 + tile] * TILE, TILE)
        return pltpu.make_async_copy(
            weights.at[:, pl.ds(column, TILE)], tiles.at[tile], sems.at[tile]
        )

    for tile in range(2 * chips):
        fetch(tile).start()
    for tile in range(2 * chips):
        cots = (mine, peer)[tile % 2]
        for number in range(4):
            grad = jnp.dot(acts[number], cots[tile // 2, number], preferred_element_type=F32)
            if number == 0:
                total[...] = grad * grad
            else:
                total[...] += grad * grad
        fetch(tile).wait()
        cols = slice(tile * TILE, (tile + 1) * TILE)
        for k in range(16):
            part = pl.ds(pl.multiple_of((mark ^ (15 - k)) * S, S), S)
            value = total[part, :]
            ref, at = (send, k) if k < 8 else (keep, k - 8)
            out = slice(at * S, (at + 1) * S)
            ref[0, out, cols] = (value * tiles[tile, part, :].astype(F32)).astype(BF)
            ref[1, out, cols] = value.astype(BF)


def fisher_parts(acts, mine, peer, weights, where, after):
    chips = mine.shape[0]
    columns = 2 * TILE * chips
    whole = pl.BlockSpec(memory_space=pltpu.VMEM)
    return pl.pallas_call(
        fisher_kernel,
        out_shape=[jax.ShapeDtypeStruct((2, ROWS // 2, columns), BF)] * 2 + [TOKEN],
        in_specs=[
            pl.BlockSpec(memory_space=pltpu.SMEM),
            whole,
            whole,
            whole,
            pl.BlockSpec(memory_space=pltpu.HBM),
            ANY,
        ],
        out_specs=[whole, whole, ANY],
        scratch_shapes=[
            pltpu.VMEM((ROWS, TILE), F32),
            pltpu.VMEM((2 * chips, ROWS, TILE), BF),
            pltpu.SemaphoreType.DMA((2 * chips,)),
        ],
        name="fisher_parts",
        **params(14),
    )(where, acts, mine, peer, weights, after)


def total_of(refs):
    total = refs[0][...].astype(F32)
    for ref in refs[1:]:
        total = total + ref[...].astype(F32)
    return total


def add_kernel(*refs):
    refs[-2][...] = total_of(refs[:-3]).astype(BF)


def merge_kernel(*refs):
    total = total_of(refs[:-3])
    refs[-2][...] = (total[0] / total[1]).astype(BF)


def add_up(parts, rows, after, divide):
    columns = parts[0][0].shape[2]
    shape = (rows, columns) if divide else (2, rows, columns)

    def block(at):
        return pl.BlockSpec((2, rows, columns), lambda i: (0, at // rows, 0))

    return pl.pallas_call(
        merge_kernel if divide else add_kernel,
        out_shape=[jax.ShapeDtypeStruct(shape, BF), TOKEN],
        grid=(1,),
        in_specs=[block(at) for _, at in parts] + [ANY],
        out_specs=[pl.BlockSpec(shape, lambda i: (0,) * len(shape)), ANY],
        name="merge" if divide else "add_up",
        **params(),
    )(*[array for array, _ in parts], after)


def join_kernel(a, b, after, out, token):
    rows = a.shape[0]
    out[:rows] = a[...]
    out[rows:] = b[...]


def join(a, b, after):
    whole = pl.BlockSpec(memory_space=pltpu.VMEM)
    return pl.pallas_call(
        join_kernel,
        out_shape=[jax.ShapeDtypeStruct((2 * a.shape[0], a.shape[1]), BF), TOKEN],
        in_specs=[whole, whole, ANY],
        out_specs=[whole, ANY],
        name="join",
        **params(),
    )(a, b, after)


def place_kernel(where, far, near, *refs):
    out = refs[-2]
    mark = where[0]
    for k in range(16):
        ref, at = (far, k) if k < 8 else (near, k - 8)
        part = pl.ds(pl.multiple_of((mark ^ (15 - k)) * S, S), S)
        out[part, :] = ref[at * S : (at + 1) * S, :]


def place(out, far, near, where, weights, after):
    block = pl.BlockSpec((ROWS // 2, TILE), lambda i, s: (0, i))
    extra = [after] if out is None else [after, out]
    return pl.pallas_call(
        place_kernel,
        out_shape=[jax.ShapeDtypeStruct(weights.shape, BF), TOKEN],
        grid_spec=pltpu.PrefetchScalarGridSpec(
            num_scalar_prefetch=1,
            grid=(far.shape[1] // TILE,),
            in_specs=[block, block] + [ANY] * len(extra),
            out_specs=[pl.BlockSpec((ROWS, TILE), lambda i, s: (0, s[1 + i])), ANY],
        ),
        input_output_aliases={} if out is None else {4: 0},
        name="place",
        **params(),
    )(where, far, near, *extra)


def on_device(activations, cotangents, checkpoints):
    y, w, v, x, c = (lax.axis_index(axis) for axis in ("y", "w", "v", "x", "c"))
    weights = checkpoints[0]
    own = cotangents[0]
    y1, y2 = bits(y, c)
    w1, _ = bits(w, c)
    mark = y1 * 8 + y2 * 4 + w1 * 2

    near = exchange(own, "x", 0)
    other = swap(own, "v")
    acts = jnp.swapaxes(activations[0], 1, 2)

    def chip(which, core):
        first = partner(x, core, 0)
        second = partner(x, core, 1)
        return (x, first, second, partner(second, core, 0))[which]

    def places(layer, pair):
        tiles = [mark]
        for which in pair:
            for core in (c, 1 - c):
                tiles.append((layer * 4 + chip(which, core)) * 2 + core)
        return jnp.stack(tiles).astype(jnp.int32)

    where = {
        "A": places(v, (0, 1)),
        "B": places(v, (2, 3)),
        "C": places(1 - v, (0, 1)),
        "D": places(1 - v, (2, 3)),
    }
    mine, peer = {}, {}
    parts = {}
    made = {}
    last, out = acts, None

    for step in ORDER:
        if step == "SA":
            mine["A"], last = stack(own, near, last)
            peer["A"] = swap(mine["A"], "c")
            mine["B"] = exchange(mine["A"], "x", 1)
            continue
        if step == "hV":
            other, last = hold(other, last)
            beyond = exchange(other, "x", 0)
            continue
        if step == "SC":
            mine["C"], last = stack(other, beyond, last)
            peer["C"] = swap(mine["C"], "c")
            mine["D"] = exchange(mine["C"], "x", 1)
            continue
        if step in ("hB", "hD"):
            name = step[1]
            mine[name], last = hold(mine[name], last)
            peer[name] = swap(mine[name], "c")
            continue
        name, stage = step[0], int(step[1])
        if stage == 7:
            out, last = place(out, *made[name], where[name], weights, last)
            continue
        if stage == 0:
            send, keep, last = fisher_parts(
                acts, mine[name], peer[name], weights, where[name], last
            )
            parts[name] = [(keep, 0)]
        elif stage < 4:
            rows, start = ((128, 0), (64, 128), (64, 192))[stage - 1]
            pairs = [(a, start - f) for a, f in parts[name]]
            send, last = add_up(pairs, rows, last, False)
        elif stage == 4:
            send, last = add_up(made[name], 64, last, True)
        else:
            send, last = join(made[name][0], made[name][1], last)
        axis, which = EXCHANGES[stage]
        came = exchange(send, axis, which)
        if stage == 0:
            parts[name].append((came, 0))
        elif stage < 3:
            parts[name].append((came, start + rows))
        elif stage == 3:
            made[name] = [(send, 0), (came, 0)]
        else:
            made[name] = [came, send]
    return out


def solution(mesh):
    fine = Mesh(mesh.devices.reshape(4, 4, 2, 4, 2), ("y", "w", "v", "x", "c"))
    mp, tp = ("y", "w"), ("v", "x", "c")
    in_specs = (P(mp, None, None, tp), P(mp, None, None, tp), P(mp, tp, None))
    return jax.shard_map(
        on_device, mesh=fine, in_specs=in_specs, out_specs=P(tp, None), check_vma=False
    )
```

```python
import functools

import jax
import jax.numpy as jnp
from jax import lax
from jax.experimental import pallas as pl
from jax.experimental.pallas import tpu as pltpu
from jax.sharding import Mesh
from jax.sharding import PartitionSpec as P

BF = jnp.bfloat16
F32 = jnp.float32
TILE = 256
ROWS = 512
S = 32
MIB = 1024 * 1024
ORDER = (
    "SA A0 hB hV",
    "SC A1 B0 A2",
    "hD C0 B1 A3",
    "D0 C1 B2 D1",
    "A4 B3 A5 D2",
    "B4 A6 C2 B5",
    "D3 C3 A7 D4",
    "B6 C4 D5 C5",
    "D6 B7 C6 D7",
    "C7",
)
ORDER = [step for line in ORDER for step in line.split()]
EXCHANGES = (
    ("y", 0),
    ("y", 1),
    ("w", 0),
    ("w", 1),
    ("w", 0),
    ("y", 1),
    ("y", 0),
)
ANY = pl.BlockSpec(memory_space=pl.ANY)
TOKEN = jax.ShapeDtypeStruct((8, 128), F32)


def partner(i, core, which):
    swap = core if which == 0 else 1 - core
    return (i ^ 1) * (1 - swap) + (3 - i) * swap


def exchange(value, axis, which):
    pairs = [
        (i * 2 + core, partner(i, core, which) * 2 + core) for i in range(4) for core in range(2)
    ]
    return lax.ppermute(value, (axis, "c"), pairs)


def swap(value, axis):
    return lax.ppermute(value, axis, [(0, 1), (1, 0)])


def bits(i, core):
    flips = (i // 2 + i) % 2, i // 2
    return (
        flips[0] * (1 - core) + flips[1] * core,
        flips[1] * (1 - core) + flips[0] * core,
    )


def params(limit=8):
    return dict(
        compiler_params=pltpu.CompilerParams(vmem_limit_bytes=limit * MIB),
        cost_estimate=pl.CostEstimate(flops=1, bytes_accessed=1, transcendentals=0),
    )


def hold_kernel(value, after, out, token):
    pass


def hold(value, after):
    return pl.pallas_call(
        hold_kernel,
        out_shape=[jax.ShapeDtypeStruct(value.shape, value.dtype), TOKEN],
        in_specs=[ANY, ANY],
        out_specs=[ANY, ANY],
        input_output_aliases={0: 0},
        name="hold",
        **params(),
    )(value, after)


def stack_kernel(a, b, after, out, token):
    out[0] = a[...]
    out[1] = b[...]


def stack(a, b, after):
    whole = pl.BlockSpec(memory_space=pltpu.VMEM)
    return pl.pallas_call(
        stack_kernel,
        out_shape=[jax.ShapeDtypeStruct((2, *a.shape), BF), TOKEN],
        in_specs=[whole, whole, ANY],
        out_specs=[whole, ANY],
        name="stack",
        **params(),
    )(a, b, after)


def fisher_kernel(where, acts, mine, peer, weights, after, send, keep, token, total, tiles, sems):
    mark = where[0]
    chips = mine.shape[0]

    def fetch(tile):
        column = pl.multiple_of(where[1 + tile] * TILE, TILE)
        return pltpu.make_async_copy(
            weights.at[:, pl.ds(column, TILE)], tiles.at[tile], sems.at[tile]
        )

    for tile in range(2 * chips):
        fetch(tile).start()
    for tile in range(2 * chips):
        cots = (mine, peer)[tile % 2]
        for number in range(4):
            grad = jnp.dot(acts[number], cots[tile // 2, number], preferred_element_type=F32)
            if number == 0:
                total[...] = grad * grad
            else:
                total[...] += grad * grad
        fetch(tile).wait()
        cols = slice(tile * TILE, (tile + 1) * TILE)
        for k in range(16):
            part = pl.ds(pl.multiple_of((mark ^ (15 - k)) * S, S), S)
            value = total[part, :]
            ref, at = (send, k) if k < 8 else (keep, k - 8)
            out = slice(at * S, (at + 1) * S)
            ref[0, out, cols] = (value * tiles[tile, part, :].astype(F32)).astype(BF)
            ref[1, out, cols] = value.astype(BF)


def fisher_parts(acts, mine, peer, weights, where, after):
    chips = mine.shape[0]
    columns = 2 * TILE * chips
    whole = pl.BlockSpec(memory_space=pltpu.VMEM)
    return pl.pallas_call(
        fisher_kernel,
        out_shape=[jax.ShapeDtypeStruct((2, ROWS // 2, columns), BF)] * 2 + [TOKEN],
        in_specs=[
            pl.BlockSpec(memory_space=pltpu.SMEM),
            whole,
            whole,
            whole,
            pl.BlockSpec(memory_space=pltpu.HBM),
            ANY,
        ],
        out_specs=[whole, whole, ANY],
        scratch_shapes=[
            pltpu.VMEM((ROWS, TILE), F32),
            pltpu.VMEM((2 * chips, ROWS, TILE), BF),
            pltpu.SemaphoreType.DMA((2 * chips,)),
        ],
        name="fisher_parts",
        **params(14),
    )(where, acts, mine, peer, pltpu.with_memory_space_constraint(weights, pltpu.HBM), after)


def total_of(refs):
    total = refs[0][...].astype(F32)
    for ref in refs[1:]:
        total = total + ref[...].astype(F32)
    return total


def add_kernel(*refs):
    refs[-2][...] = total_of(refs[:-3]).astype(BF)


def merge_kernel(*refs):
    total = total_of(refs[:-3])
    refs[-2][...] = (total[0] / total[1]).astype(BF)


def add_up(parts, rows, after, divide):
    columns = parts[0][0].shape[2]
    shape = (rows, columns) if divide else (2, rows, columns)

    def block(at):
        return pl.BlockSpec((2, rows, columns), lambda i: (0, at // rows, 0))

    return pl.pallas_call(
        merge_kernel if divide else add_kernel,
        out_shape=[jax.ShapeDtypeStruct(shape, BF), TOKEN],
        grid=(1,),
        in_specs=[block(at) for _, at in parts] + [ANY],
        out_specs=[pl.BlockSpec(shape, lambda i: (0,) * len(shape)), ANY],
        name="merge" if divide else "add_up",
        **params(),
    )(*[array for array, _ in parts], after)


def join_kernel(a, b, after, out, token):
    rows = a.shape[0]
    out[:rows] = a[...]
    out[rows:] = b[...]


def join(a, b, after):
    whole = pl.BlockSpec(memory_space=pltpu.VMEM)
    return pl.pallas_call(
        join_kernel,
        out_shape=[jax.ShapeDtypeStruct((2 * a.shape[0], a.shape[1]), BF), TOKEN],
        in_specs=[whole, whole, ANY],
        out_specs=[whole, ANY],
        name="join",
        **params(),
    )(a, b, after)


def place_kernel(where, far, near, *refs):
    out = refs[-2]
    mark = where[0]
    for k in range(16):
        ref, at = (far, k) if k < 8 else (near, k - 8)
        part = pl.ds(pl.multiple_of((mark ^ (15 - k)) * S, S), S)
        out[part, :] = ref[at * S : (at + 1) * S, :]


def place(out, far, near, where, weights, after):
    block = pl.BlockSpec((ROWS // 2, TILE), lambda i, s: (0, i))
    extra = [after] if out is None else [after, out]
    return pl.pallas_call(
        place_kernel,
        out_shape=[jax.ShapeDtypeStruct(weights.shape, BF), TOKEN],
        grid_spec=pltpu.PrefetchScalarGridSpec(
            num_scalar_prefetch=1,
            grid=(far.shape[1] // TILE,),
            in_specs=[block, block] + [ANY] * len(extra),
            out_specs=[pl.BlockSpec((ROWS, TILE), lambda i, s: (0, s[1 + i])), ANY],
        ),
        input_output_aliases={} if out is None else {4: 0},
        name="place",
        **params(),
    )(where, far, near, *extra)


def on_device(activations, cotangents, checkpoints):
    y, w, v, x, c = (lax.axis_index(axis) for axis in ("y", "w", "v", "x", "c"))
    weights = checkpoints[0]
    own = cotangents[0]
    y1, y2 = bits(y, c)
    w1, _ = bits(w, c)
    mark = y1 * 8 + y2 * 4 + w1 * 2

    near = exchange(own, "x", 0)
    other = swap(own, "v")
    acts = jnp.swapaxes(activations[0], 1, 2)

    def chip(which, core):
        first = partner(x, core, 0)
        second = partner(x, core, 1)
        return (x, first, second, partner(second, core, 0))[which]

    def places(layer, pair):
        tiles = [mark]
        for which in pair:
            for core in (c, 1 - c):
                tiles.append((layer * 4 + chip(which, core)) * 2 + core)
        return jnp.stack(tiles).astype(jnp.int32)

    where = {
        "A": places(v, (0, 1)),
        "B": places(v, (2, 3)),
        "C": places(1 - v, (0, 1)),
        "D": places(1 - v, (2, 3)),
    }
    mine, peer = {}, {}
    parts = {}
    made = {}
    last, out = acts, None

    for step in ORDER:
        if step == "SA":
            mine["A"], last = stack(own, near, last)
            peer["A"] = swap(mine["A"], "c")
            mine["B"] = exchange(mine["A"], "x", 1)
            continue
        if step == "hV":
            other, last = hold(other, last)
            beyond = exchange(other, "x", 0)
            continue
        if step == "SC":
            mine["C"], last = stack(other, beyond, last)
            peer["C"] = swap(mine["C"], "c")
            mine["D"] = exchange(mine["C"], "x", 1)
            continue
        if step in ("hB", "hD"):
            name = step[1]
            mine[name], last = hold(mine[name], last)
            peer[name] = swap(mine[name], "c")
            continue
        name, stage = step[0], int(step[1])
        if stage == 7:
            out, last = place(out, *made[name], where[name], weights, last)
            continue
        if stage == 0:
            send, keep, last = fisher_parts(
                acts, mine[name], peer[name], weights, where[name], last
            )
            parts[name] = [(keep, 0)]
        elif stage < 4:
            rows, start = ((128, 0), (64, 128), (64, 192))[stage - 1]
            pairs = [(a, start - f) for a, f in parts[name]]
            send, last = add_up(pairs, rows, last, False)
        elif stage == 4:
            send, last = add_up(made[name], 64, last, True)
        else:
            send, last = join(made[name][0], made[name][1], last)
        axis, which = EXCHANGES[stage]
        came = exchange(send, axis, which)
        if stage == 0:
            parts[name].append((came, 0))
        elif stage < 3:
            parts[name].append((came, start + rows))
        elif stage == 3:
            made[name] = [(send, 0), (came, 0)]
        else:
            made[name] = [came, send]
    return out


def solution(mesh):
    fine = Mesh(mesh.devices.reshape(4, 4, 2, 4, 2), ("y", "w", "v", "x", "c"))
    mp, tp = ("y", "w"), ("v", "x", "c")
    in_specs = (P(mp, None, None, tp), P(mp, None, None, tp), P(mp, tp, None))
    return jax.shard_map(
        on_device, mesh=fine, in_specs=in_specs, out_specs=P(tp, None), check_vma=False
    )
```

```python
import functools

import jax
import jax.numpy as jnp
from jax import lax
from jax.experimental import pallas as pl
from jax.experimental.pallas import tpu as pltpu
from jax.sharding import Mesh
from jax.sharding import PartitionSpec as P

BF = jnp.bfloat16
F32 = jnp.float32
TILE = 256
ROWS = 512
S = 32
MIB = 1024 * 1024
ORDER = (
    "SA A0 hB hV",
    "SC A1 B0 A2",
    "hD C0 B1 A3",
    "D0 C1 B2 D1",
    "A4 B3 A5 D2",
    "B4 A6 C2 B5",
    "D3 C3 A7 D4",
    "B6 C4 D5 C5",
    "D6 B7 C6 D7",
    "C7",
)
ORDER = [step for line in ORDER for step in line.split()]
EXCHANGES = (
    ("y", 0),
    ("y", 1),
    ("w", 0),
    ("w", 1),
    ("w", 0),
    ("y", 1),
    ("y", 0),
)
ANY = pl.BlockSpec(memory_space=pl.ANY)
TOKEN = jax.ShapeDtypeStruct((8, 128), F32)


def partner(i, core, which):
    swap = core if which == 0 else 1 - core
    return (i ^ 1) * (1 - swap) + (3 - i) * swap


def exchange(value, axis, which):
    pairs = [
        (i * 2 + core, partner(i, core, which) * 2 + core) for i in range(4) for core in range(2)
    ]
    return lax.ppermute(value, (axis, "c"), pairs)


def swap(value, axis):
    return lax.ppermute(value, axis, [(0, 1), (1, 0)])


def bits(i, core):
    flips = (i // 2 + i) % 2, i // 2
    return (
        flips[0] * (1 - core) + flips[1] * core,
        flips[1] * (1 - core) + flips[0] * core,
    )


def params(limit=8):
    return dict(
        compiler_params=pltpu.CompilerParams(vmem_limit_bytes=limit * MIB),
        cost_estimate=pl.CostEstimate(flops=1, bytes_accessed=1, transcendentals=0),
    )


def hold_kernel(value, after, out, token):
    pass


def hold(value, after):
    return pl.pallas_call(
        hold_kernel,
        out_shape=[jax.ShapeDtypeStruct(value.shape, value.dtype), TOKEN],
        in_specs=[ANY, ANY],
        out_specs=[ANY, ANY],
        input_output_aliases={0: 0},
        name="hold",
        **params(),
    )(value, after)


def stack_kernel(a, b, after, out, token, sems):
    copies = [
        pltpu.make_async_copy(ref, out.at[at], sems.at[at]) for at, ref in enumerate((a, b))
    ]
    for copy in copies:
        copy.start()
    for copy in copies:
        copy.wait()


def stack(a, b, after):
    return pl.pallas_call(
        stack_kernel,
        out_shape=[jax.ShapeDtypeStruct((2, *a.shape), BF), TOKEN],
        in_specs=[ANY, ANY, ANY],
        out_specs=[ANY, ANY],
        scratch_shapes=[pltpu.SemaphoreType.DMA((2,))],
        name="stack",
        **params(),
    )(a, b, after)


def fisher_kernel(where, acts, mine, peer, weights, after, send, keep, token, total, tiles, sems):
    mark = where[0]
    chips = mine.shape[0]

    def fetch(tile):
        column = pl.multiple_of(where[1 + tile] * TILE, TILE)
        return pltpu.make_async_copy(
            weights.at[:, pl.ds(column, TILE)], tiles.at[tile], sems.at[tile]
        )

    for tile in range(2 * chips):
        fetch(tile).start()
    for tile in range(2 * chips):
        cots = (mine, peer)[tile % 2]
        for number in range(4):
            grad = jnp.dot(acts[number], cots[tile // 2, number], preferred_element_type=F32)
            if number == 0:
                total[...] = grad * grad
            else:
                total[...] += grad * grad
        fetch(tile).wait()
        cols = slice(tile * TILE, (tile + 1) * TILE)
        for k in range(16):
            part = pl.ds(pl.multiple_of((mark ^ (15 - k)) * S, S), S)
            value = total[part, :]
            ref, at = (send, k) if k < 8 else (keep, k - 8)
            out = slice(at * S, (at + 1) * S)
            ref[0, out, cols] = (value * tiles[tile, part, :].astype(F32)).astype(BF)
            ref[1, out, cols] = value.astype(BF)


def fisher_parts(acts, mine, peer, weights, where, after):
    chips = mine.shape[0]
    columns = 2 * TILE * chips
    whole = pl.BlockSpec(memory_space=pltpu.VMEM)
    return pl.pallas_call(
        fisher_kernel,
        out_shape=[jax.ShapeDtypeStruct((2, ROWS // 2, columns), BF)] * 2 + [TOKEN],
        in_specs=[
            pl.BlockSpec(memory_space=pltpu.SMEM),
            whole,
            whole,
            whole,
            pl.BlockSpec(memory_space=pltpu.HBM),
            ANY,
        ],
        out_specs=[whole, whole, ANY],
        scratch_shapes=[
            pltpu.VMEM((ROWS, TILE), F32),
            pltpu.VMEM((2 * chips, ROWS, TILE), BF),
            pltpu.SemaphoreType.DMA((2 * chips,)),
        ],
        name="fisher_parts",
        **params(14),
    )(where, acts, mine, peer, pltpu.with_memory_space_constraint(weights, pltpu.HBM), after)


def total_of(refs):
    total = refs[0][...].astype(F32)
    for ref in refs[1:]:
        total = total + ref[...].astype(F32)
    return total


def add_kernel(*refs):
    refs[-2][...] = total_of(refs[:-3]).astype(BF)


def merge_kernel(*refs):
    total = total_of(refs[:-3])
    refs[-2][...] = (total[0] / total[1]).astype(BF)


def add_up(parts, rows, after, divide):
    columns = parts[0][0].shape[2]
    shape = (rows, columns) if divide else (2, rows, columns)

    def block(at):
        return pl.BlockSpec((2, rows, columns), lambda i: (0, at // rows, 0))

    return pl.pallas_call(
        merge_kernel if divide else add_kernel,
        out_shape=[jax.ShapeDtypeStruct(shape, BF), TOKEN],
        grid=(1,),
        in_specs=[block(at) for _, at in parts] + [ANY],
        out_specs=[pl.BlockSpec(shape, lambda i: (0,) * len(shape)), ANY],
        name="merge" if divide else "add_up",
        **params(),
    )(*[array for array, _ in parts], after)


def join_kernel(a, b, after, out, token):
    rows = a.shape[0]
    out[:rows] = a[...]
    out[rows:] = b[...]


def join(a, b, after):
    whole = pl.BlockSpec(memory_space=pltpu.VMEM)
    return pl.pallas_call(
        join_kernel,
        out_shape=[jax.ShapeDtypeStruct((2 * a.shape[0], a.shape[1]), BF), TOKEN],
        in_specs=[whole, whole, ANY],
        out_specs=[whole, ANY],
        name="join",
        **params(),
    )(a, b, after)


def place_kernel(where, far, near, *refs):
    out, _, tiles, sems = refs[-4:]
    mark = where[0]
    count = tiles.shape[0]

    def store(tile):
        column = pl.multiple_of(where[1 + tile] * TILE, TILE)
        return pltpu.make_async_copy(
            tiles.at[tile], out.at[:, pl.ds(column, TILE)], sems.at[tile]
        )

    for tile in range(count):
        cols = slice(tile * TILE, (tile + 1) * TILE)
        for k in range(16):
            ref, at = (far, k) if k < 8 else (near, k - 8)
            part = pl.ds(pl.multiple_of((mark ^ (15 - k)) * S, S), S)
            tiles[tile, part, :] = ref[at * S : (at + 1) * S, cols]
        store(tile).start()
    for tile in range(count):
        store(tile).wait()


def place(out, far, near, where, weights, after):
    whole = pl.BlockSpec(memory_space=pltpu.VMEM)
    count = far.shape[1] // TILE
    extra = [after] if out is None else [after, out]
    return pl.pallas_call(
        place_kernel,
        out_shape=[jax.ShapeDtypeStruct(weights.shape, BF), TOKEN],
        in_specs=[pl.BlockSpec(memory_space=pltpu.SMEM), whole, whole] + [ANY] * len(extra),
        out_specs=[ANY, ANY],
        scratch_shapes=[
            pltpu.VMEM((count, ROWS, TILE), BF),
            pltpu.SemaphoreType.DMA((count,)),
        ],
        input_output_aliases={} if out is None else {4: 0},
        name="place",
        **params(),
    )(where, far, near, *extra)


def on_device(activations, cotangents, checkpoints):
    y, w, v, x, c = (lax.axis_index(axis) for axis in ("y", "w", "v", "x", "c"))
    weights = checkpoints[0]
    own = cotangents[0]
    y1, y2 = bits(y, c)
    w1, _ = bits(w, c)
    mark = y1 * 8 + y2 * 4 + w1 * 2

    near = exchange(own, "x", 0)
    other = swap(own, "v")
    acts = jnp.swapaxes(activations[0], 1, 2)

    def chip(which, core):
        first = partner(x, core, 0)
        second = partner(x, core, 1)
        return (x, first, second, partner(second, core, 0))[which]

    def places(layer, pair):
        tiles = [mark]
        for which in pair:
            for core in (c, 1 - c):
                tiles.append((layer * 4 + chip(which, core)) * 2 + core)
        return jnp.stack(tiles).astype(jnp.int32)

    where = {
        "A": places(v, (0, 1)),
        "B": places(v, (2, 3)),
        "C": places(1 - v, (0, 1)),
        "D": places(1 - v, (2, 3)),
    }
    mine, peer = {}, {}
    parts = {}
    made = {}
    last, out = acts, None

    for step in ORDER:
        if step == "SA":
            mine["A"], last = stack(own, near, last)
            peer["A"] = swap(mine["A"], "c")
            mine["B"] = exchange(mine["A"], "x", 1)
            continue
        if step == "hV":
            other, last = hold(other, last)
            beyond = exchange(other, "x", 0)
            continue
        if step == "SC":
            mine["C"], last = stack(other, beyond, last)
            peer["C"] = swap(mine["C"], "c")
            mine["D"] = exchange(mine["C"], "x", 1)
            continue
        if step in ("hB", "hD"):
            name = step[1]
            mine[name], last = hold(mine[name], last)
            peer[name] = swap(mine[name], "c")
            continue
        name, stage = step[0], int(step[1])
        if stage == 7:
            out, last = place(out, *made[name], where[name], weights, last)
            continue
        if stage == 0:
            send, keep, last = fisher_parts(
                acts, mine[name], peer[name], weights, where[name], last
            )
            parts[name] = [(keep, 0)]
        elif stage < 4:
            rows, start = ((128, 0), (64, 128), (64, 192))[stage - 1]
            pairs = [(a, start - f) for a, f in parts[name]]
            send, last = add_up(pairs, rows, last, False)
        elif stage == 4:
            send, last = add_up(made[name], 64, last, True)
        else:
            send, last = join(made[name][0], made[name][1], last)
        axis, which = EXCHANGES[stage]
        came = exchange(send, axis, which)
        if stage == 0:
            parts[name].append((came, 0))
        elif stage < 3:
            parts[name].append((came, start + rows))
        elif stage == 3:
            made[name] = [(send, 0), (came, 0)]
        else:
            made[name] = [came, send]
    return out


def solution(mesh):
    fine = Mesh(mesh.devices.reshape(4, 4, 2, 4, 2), ("y", "w", "v", "x", "c"))
    mp, tp = ("y", "w"), ("v", "x", "c")
    in_specs = (P(mp, None, None, tp), P(mp, None, None, tp), P(mp, tp, None))
    return jax.shard_map(
        on_device, mesh=fine, in_specs=in_specs, out_specs=P(tp, None), check_vma=False
    )
```

```python
import functools

import jax
import jax.numpy as jnp
from jax import lax
from jax.experimental import pallas as pl
from jax.experimental.pallas import tpu as pltpu
from jax.sharding import Mesh
from jax.sharding import PartitionSpec as P

BF = jnp.bfloat16
F32 = jnp.float32
TILE = 256
ROWS = 512
S = 32
MIB = 1024 * 1024
ORDER = (
    "SA A0 hB hV",
    "SC A1 B0 A2",
    "hD C0 B1 A3",
    "D0 C1 B2 D1",
    "A4 B3 A5 D2",
    "B4 A6 C2 B5",
    "D3 C3 A7 D4",
    "B6 C4 D5 C5",
    "D6 B7 C6 D7",
    "C7",
)
ORDER = [step for line in ORDER for step in line.split()]
EXCHANGES = (
    ("y", 0),
    ("y", 1),
    ("w", 0),
    ("w", 1),
    ("w", 0),
    ("y", 1),
    ("y", 0),
)
ANY = pl.BlockSpec(memory_space=pl.ANY)
TOKEN = jax.ShapeDtypeStruct((8, 128), F32)


def partner(i, core, which):
    swap = core if which == 0 else 1 - core
    return (i ^ 1) * (1 - swap) + (3 - i) * swap


def exchange(value, axis, which):
    pairs = [
        (i * 2 + core, partner(i, core, which) * 2 + core) for i in range(4) for core in range(2)
    ]
    return lax.ppermute(value, (axis, "c"), pairs)


def swap(value, axis):
    return lax.ppermute(value, axis, [(0, 1), (1, 0)])


def bits(i, core):
    flips = (i // 2 + i) % 2, i // 2
    return (
        flips[0] * (1 - core) + flips[1] * core,
        flips[1] * (1 - core) + flips[0] * core,
    )


def params(limit=8):
    return dict(
        compiler_params=pltpu.CompilerParams(vmem_limit_bytes=limit * MIB),
        cost_estimate=pl.CostEstimate(flops=1, bytes_accessed=1, transcendentals=0),
    )


def hold_kernel(value, after, out, token):
    pass


def hold(value, after):
    return pl.pallas_call(
        hold_kernel,
        out_shape=[jax.ShapeDtypeStruct(value.shape, value.dtype), TOKEN],
        in_specs=[ANY, ANY],
        out_specs=[ANY, ANY],
        input_output_aliases={0: 0},
        name="hold",
        **params(),
    )(value, after)


def stack_kernel(a, b, after, out, token):
    out[0] = a[...]
    out[1] = b[...]


def stack(a, b, after):
    whole = pl.BlockSpec(memory_space=pltpu.VMEM)
    return pl.pallas_call(
        stack_kernel,
        out_shape=[jax.ShapeDtypeStruct((2, *a.shape), BF), TOKEN],
        in_specs=[whole, whole, ANY],
        out_specs=[whole, ANY],
        name="stack",
        **params(),
    )(a, b, after)


def fisher_kernel(where, acts, mine, peer, weights, after, send, keep, token, total, tiles, sems):
    mark = where[0]
    chips = mine.shape[0]

    def fetch(tile):
        column = pl.multiple_of(where[1 + tile] * TILE, TILE)
        return pltpu.make_async_copy(
            weights.at[:, pl.ds(column, TILE)], tiles.at[tile], sems.at[tile]
        )

    for tile in range(2 * chips):
        fetch(tile).start()
    for tile in range(2 * chips):
        cots = (mine, peer)[tile % 2]
        for number in range(4):
            grad = jnp.dot(acts[number], cots[tile // 2, number], preferred_element_type=F32)
            if number == 0:
                total[...] = grad * grad
            else:
                total[...] += grad * grad
        fetch(tile).wait()
        cols = slice(tile * TILE, (tile + 1) * TILE)
        for k in range(16):
            part = pl.ds(pl.multiple_of((mark ^ (15 - k)) * S, S), S)
            value = total[part, :]
            ref, at = (send, k) if k < 8 else (keep, k - 8)
            out = slice(at * S, (at + 1) * S)
            ref[0, out, cols] = (value * tiles[tile, part, :].astype(F32)).astype(BF)
            ref[1, out, cols] = value.astype(BF)


def fisher_parts(acts, mine, peer, weights, where, after):
    chips = mine.shape[0]
    columns = 2 * TILE * chips
    whole = pl.BlockSpec(memory_space=pltpu.VMEM)
    return pl.pallas_call(
        fisher_kernel,
        out_shape=[jax.ShapeDtypeStruct((2, ROWS // 2, columns), BF)] * 2 + [TOKEN],
        in_specs=[
            pl.BlockSpec(memory_space=pltpu.SMEM),
            whole,
            whole,
            whole,
            pl.BlockSpec(memory_space=pltpu.HBM),
            ANY,
        ],
        out_specs=[whole, whole, ANY],
        scratch_shapes=[
            pltpu.VMEM((ROWS, TILE), F32),
            pltpu.VMEM((2 * chips, ROWS, TILE), BF),
            pltpu.SemaphoreType.DMA((2 * chips,)),
        ],
        name="fisher_parts",
        **params(14),
    )(where, acts, mine, peer, pltpu.with_memory_space_constraint(weights, pltpu.HBM), after)


def total_of(refs):
    total = refs[0][...].astype(F32)
    for ref in refs[1:]:
        total = total + ref[...].astype(F32)
    return total


def add_kernel(*refs):
    refs[-2][...] = total_of(refs[:-3]).astype(BF)


def merge_kernel(*refs):
    total = total_of(refs[:-3])
    refs[-2][...] = (total[0] / total[1]).astype(BF)


def add_up(parts, rows, after, divide):
    columns = parts[0][0].shape[2]
    shape = (rows, columns) if divide else (2, rows, columns)

    def block(at):
        return pl.BlockSpec((2, rows, columns), lambda i: (0, at // rows, 0))

    return pl.pallas_call(
        merge_kernel if divide else add_kernel,
        out_shape=[jax.ShapeDtypeStruct(shape, BF), TOKEN],
        grid=(1,),
        in_specs=[block(at) for _, at in parts] + [ANY],
        out_specs=[pl.BlockSpec(shape, lambda i: (0,) * len(shape)), ANY],
        name="merge" if divide else "add_up",
        **params(),
    )(*[array for array, _ in parts], after)


def join_kernel(a, b, after, out, token):
    rows = a.shape[0]
    out[:rows] = a[...]
    out[rows:] = b[...]


def join(a, b, after):
    whole = pl.BlockSpec(memory_space=pltpu.VMEM)
    return pl.pallas_call(
        join_kernel,
        out_shape=[jax.ShapeDtypeStruct((2 * a.shape[0], a.shape[1]), BF), TOKEN],
        in_specs=[whole, whole, ANY],
        out_specs=[whole, ANY],
        name="join",
        **params(),
    )(a, b, after)


def place_kernel(where, far, near, *refs):
    out, _, tiles, sems = refs[-4:]
    mark = where[0]
    count = tiles.shape[0]

    def store(tile):
        column = pl.multiple_of(where[1 + tile] * TILE, TILE)
        return pltpu.make_async_copy(
            tiles.at[tile], out.at[:, pl.ds(column, TILE)], sems.at[tile]
        )

    for tile in range(count):
        cols = slice(tile * TILE, (tile + 1) * TILE)
        for k in range(16):
            ref, at = (far, k) if k < 8 else (near, k - 8)
            part = pl.ds(pl.multiple_of((mark ^ (15 - k)) * S, S), S)
            tiles[tile, part, :] = ref[at * S : (at + 1) * S, cols]
        store(tile).start()
    for tile in range(count):
        store(tile).wait()


def place(out, far, near, where, weights, after):
    whole = pl.BlockSpec(memory_space=pltpu.VMEM)
    count = far.shape[1] // TILE
    extra = [after] if out is None else [after, out]
    return pl.pallas_call(
        place_kernel,
        out_shape=[jax.ShapeDtypeStruct(weights.shape, BF), TOKEN],
        in_specs=[pl.BlockSpec(memory_space=pltpu.SMEM), whole, whole] + [ANY] * len(extra),
        out_specs=[ANY, ANY],
        scratch_shapes=[
            pltpu.VMEM((count, ROWS, TILE), BF),
            pltpu.SemaphoreType.DMA((count,)),
        ],
        input_output_aliases={} if out is None else {4: 0},
        name="place",
        **params(),
    )(where, far, near, *extra)


def on_device(activations, cotangents, checkpoints):
    y, w, v, x, c = (lax.axis_index(axis) for axis in ("y", "w", "v", "x", "c"))
    weights = checkpoints[0]
    own = cotangents[0]
    y1, y2 = bits(y, c)
    w1, _ = bits(w, c)
    mark = y1 * 8 + y2 * 4 + w1 * 2

    near = exchange(own, "x", 0)
    other = swap(own, "v")
    acts = jnp.swapaxes(activations[0], 1, 2)

    def chip(which, core):
        first = partner(x, core, 0)
        second = partner(x, core, 1)
        return (x, first, second, partner(second, core, 0))[which]

    def places(layer, pair):
        tiles = [mark]
        for which in pair:
            for core in (c, 1 - c):
                tiles.append((layer * 4 + chip(which, core)) * 2 + core)
        return jnp.stack(tiles).astype(jnp.int32)

    where = {
        "A": places(v, (0, 1)),
        "B": places(v, (2, 3)),
        "C": places(1 - v, (0, 1)),
        "D": places(1 - v, (2, 3)),
    }
    mine, peer = {}, {}
    parts = {}
    made = {}
    last, out = acts, None

    for step in ORDER:
        if step == "SA":
            mine["A"], last = stack(own, near, last)
            peer["A"] = swap(mine["A"], "c")
            mine["B"] = exchange(mine["A"], "x", 1)
            continue
        if step == "hV":
            other, last = hold(other, last)
            beyond = exchange(other, "x", 0)
            continue
        if step == "SC":
            mine["C"], last = stack(other, beyond, last)
            peer["C"] = swap(mine["C"], "c")
            mine["D"] = exchange(mine["C"], "x", 1)
            continue
        if step in ("hB", "hD"):
            name = step[1]
            mine[name], last = hold(mine[name], last)
            peer[name] = swap(mine[name], "c")
            continue
        name, stage = step[0], int(step[1])
        if stage == 7:
            out, last = place(out, *made[name], where[name], weights, last)
            continue
        if stage == 0:
            send, keep, last = fisher_parts(
                acts, mine[name], peer[name], weights, where[name], last
            )
            parts[name] = [(keep, 0)]
        elif stage < 4:
            rows, start = ((128, 0), (64, 128), (64, 192))[stage - 1]
            pairs = [(a, start - f) for a, f in parts[name]]
            send, last = add_up(pairs, rows, last, False)
        elif stage == 4:
            send, last = add_up(made[name], 64, last, True)
        else:
            send, last = join(made[name][0], made[name][1], last)
        axis, which = EXCHANGES[stage]
        came = exchange(send, axis, which)
        if stage == 0:
            parts[name].append((came, 0))
        elif stage < 3:
            parts[name].append((came, start + rows))
        elif stage == 3:
            made[name] = [(send, 0), (came, 0)]
        else:
            made[name] = [came, send]
    return out


def solution(mesh):
    fine = Mesh(mesh.devices.reshape(4, 4, 2, 4, 2), ("y", "w", "v", "x", "c"))
    mp, tp = ("y", "w"), ("v", "x", "c")
    in_specs = (P(mp, None, None, tp), P(mp, None, None, tp), P(mp, tp, None))
    return jax.shard_map(
        on_device, mesh=fine, in_specs=in_specs, out_specs=P(tp, None), check_vma=False
    )
```

```python
import functools

import jax
import jax.numpy as jnp
from jax import lax
from jax.experimental import pallas as pl
from jax.experimental.pallas import tpu as pltpu
from jax.sharding import Mesh
from jax.sharding import PartitionSpec as P

BF = jnp.bfloat16
F32 = jnp.float32
TILE = 256
ROWS = 512
S = 32
MIB = 1024 * 1024
ORDER = (
    "SA A0 hB hV",
    "SC A1 B0 A2",
    "hD C0 B1 A3",
    "D0 C1 B2 D1",
    "A4 B3 A5 D2",
    "B4 A6 C2 B5",
    "D3 C3 A7 D4",
    "B6 C4 D5 C5",
    "D6 B7 C6 D7",
    "C7",
)
ORDER = [step for line in ORDER for step in line.split()]
EXCHANGES = (
    ("y", 0),
    ("y", 1),
    ("w", 0),
    ("w", 1),
    ("w", 0),
    ("y", 1),
    ("y", 0),
)
ANY = pl.BlockSpec(memory_space=pl.ANY)
TOKEN = jax.ShapeDtypeStruct((8, 128), F32)


def partner(i, core, which):
    swap = core if which == 0 else 1 - core
    return (i ^ 1) * (1 - swap) + (3 - i) * swap


def exchange(value, axis, which):
    pairs = [
        (i * 2 + core, partner(i, core, which) * 2 + core) for i in range(4) for core in range(2)
    ]
    return lax.ppermute(value, (axis, "c"), pairs)


def swap(value, axis):
    return lax.ppermute(value, axis, [(0, 1), (1, 0)])


def bits(i, core):
    flips = (i // 2 + i) % 2, i // 2
    return (
        flips[0] * (1 - core) + flips[1] * core,
        flips[1] * (1 - core) + flips[0] * core,
    )


def params(limit=8):
    return dict(
        compiler_params=pltpu.CompilerParams(vmem_limit_bytes=limit * MIB),
        cost_estimate=pl.CostEstimate(flops=1, bytes_accessed=1, transcendentals=0),
    )


def hold_kernel(value, after, out, token):
    pass


def hold(value, after):
    return pl.pallas_call(
        hold_kernel,
        out_shape=[jax.ShapeDtypeStruct(value.shape, value.dtype), TOKEN],
        in_specs=[ANY, ANY],
        out_specs=[ANY, ANY],
        input_output_aliases={0: 0},
        name="hold",
        **params(),
    )(value, after)


def stack_kernel(a, b, after, out, token):
    out[0] = a[...]
    out[1] = b[...]


def stack(a, b, after):
    whole = pl.BlockSpec(memory_space=pltpu.VMEM)
    return pl.pallas_call(
        stack_kernel,
        out_shape=[jax.ShapeDtypeStruct((2, *a.shape), BF), TOKEN],
        in_specs=[whole, whole, ANY],
        out_specs=[whole, ANY],
        name="stack",
        **params(),
    )(a, b, after)


def fisher_kernel(where, acts, mine, peer, weights, after, send, keep, token, total, tiles, sems):
    mark = where[0]
    chips = mine.shape[0]

    def fetch(tile):
        column = pl.multiple_of(where[1 + tile] * TILE, TILE)
        return pltpu.make_async_copy(
            weights.at[:, pl.ds(column, TILE)], tiles.at[tile], sems.at[tile]
        )

    for tile in range(2 * chips):
        fetch(tile).start()
    for tile in range(2 * chips):
        cots = (mine, peer)[tile % 2]
        squares = None
        for number in range(4):
            grad = jnp.dot(acts[number], cots[tile // 2, number], preferred_element_type=F32)
            squares = grad * grad if squares is None else squares + grad * grad
        total[...] = squares
        fetch(tile).wait()
        cols = slice(tile * TILE, (tile + 1) * TILE)
        for k in range(16):
            part = pl.ds(pl.multiple_of((mark ^ (15 - k)) * S, S), S)
            value = total[part, :]
            ref, at = (send, k) if k < 8 else (keep, k - 8)
            out = slice(at * S, (at + 1) * S)
            ref[0, out, cols] = (value * tiles[tile, part, :].astype(F32)).astype(BF)
            ref[1, out, cols] = value.astype(BF)


def fisher_parts(acts, mine, peer, weights, where, after):
    chips = mine.shape[0]
    columns = 2 * TILE * chips
    whole = pl.BlockSpec(memory_space=pltpu.VMEM)
    return pl.pallas_call(
        fisher_kernel,
        out_shape=[jax.ShapeDtypeStruct((2, ROWS // 2, columns), BF)] * 2 + [TOKEN],
        in_specs=[
            pl.BlockSpec(memory_space=pltpu.SMEM),
            whole,
            whole,
            whole,
            pl.BlockSpec(memory_space=pltpu.HBM),
            ANY,
        ],
        out_specs=[whole, whole, ANY],
        scratch_shapes=[
            pltpu.VMEM((ROWS, TILE), F32),
            pltpu.VMEM((2 * chips, ROWS, TILE), BF),
            pltpu.SemaphoreType.DMA((2 * chips,)),
        ],
        name="fisher_parts",
        **params(14),
    )(where, acts, mine, peer, pltpu.with_memory_space_constraint(weights, pltpu.HBM), after)


def total_of(refs):
    total = refs[0][...].astype(F32)
    for ref in refs[1:]:
        total = total + ref[...].astype(F32)
    return total


def add_kernel(*refs):
    refs[-2][...] = total_of(refs[:-3]).astype(BF)


def merge_kernel(*refs):
    total = total_of(refs[:-3])
    refs[-2][...] = (total[0] / total[1]).astype(BF)


def add_up(parts, rows, after, divide):
    columns = parts[0][0].shape[2]
    shape = (rows, columns) if divide else (2, rows, columns)

    def block(at):
        return pl.BlockSpec((2, rows, columns), lambda i: (0, at // rows, 0))

    return pl.pallas_call(
        merge_kernel if divide else add_kernel,
        out_shape=[jax.ShapeDtypeStruct(shape, BF), TOKEN],
        grid=(1,),
        in_specs=[block(at) for _, at in parts] + [ANY],
        out_specs=[pl.BlockSpec(shape, lambda i: (0,) * len(shape)), ANY],
        name="merge" if divide else "add_up",
        **params(),
    )(*[array for array, _ in parts], after)


def join_kernel(a, b, after, out, token):
    rows = a.shape[0]
    out[:rows] = a[...]
    out[rows:] = b[...]


def join(a, b, after):
    whole = pl.BlockSpec(memory_space=pltpu.VMEM)
    return pl.pallas_call(
        join_kernel,
        out_shape=[jax.ShapeDtypeStruct((2 * a.shape[0], a.shape[1]), BF), TOKEN],
        in_specs=[whole, whole, ANY],
        out_specs=[whole, ANY],
        name="join",
        **params(),
    )(a, b, after)


def place_kernel(where, far, near, *refs):
    out, _, tiles, sems = refs[-4:]
    mark = where[0]
    count = tiles.shape[0]

    def store(tile):
        column = pl.multiple_of(where[1 + tile] * TILE, TILE)
        return pltpu.make_async_copy(
            tiles.at[tile], out.at[:, pl.ds(column, TILE)], sems.at[tile]
        )

    for tile in range(count):
        cols = slice(tile * TILE, (tile + 1) * TILE)
        for k in range(16):
            ref, at = (far, k) if k < 8 else (near, k - 8)
            part = pl.ds(pl.multiple_of((mark ^ (15 - k)) * S, S), S)
            tiles[tile, part, :] = ref[at * S : (at + 1) * S, cols]
        store(tile).start()
    for tile in range(count):
        store(tile).wait()


def place(out, far, near, where, weights, after):
    whole = pl.BlockSpec(memory_space=pltpu.VMEM)
    count = far.shape[1] // TILE
    extra = [after] if out is None else [after, out]
    return pl.pallas_call(
        place_kernel,
        out_shape=[jax.ShapeDtypeStruct(weights.shape, BF), TOKEN],
        in_specs=[pl.BlockSpec(memory_space=pltpu.SMEM), whole, whole] + [ANY] * len(extra),
        out_specs=[ANY, ANY],
        scratch_shapes=[
            pltpu.VMEM((count, ROWS, TILE), BF),
            pltpu.SemaphoreType.DMA((count,)),
        ],
        input_output_aliases={} if out is None else {4: 0},
        name="place",
        **params(),
    )(where, far, near, *extra)


def on_device(activations, cotangents, checkpoints):
    y, w, v, x, c = (lax.axis_index(axis) for axis in ("y", "w", "v", "x", "c"))
    weights = checkpoints[0]
    own = cotangents[0]
    y1, y2 = bits(y, c)
    w1, _ = bits(w, c)
    mark = y1 * 8 + y2 * 4 + w1 * 2

    near = exchange(own, "x", 0)
    other = swap(own, "v")
    acts = jnp.swapaxes(activations[0], 1, 2)

    def chip(which, core):
        first = partner(x, core, 0)
        second = partner(x, core, 1)
        return (x, first, second, partner(second, core, 0))[which]

    def places(layer, pair):
        tiles = [mark]
        for which in pair:
            for core in (c, 1 - c):
                tiles.append((layer * 4 + chip(which, core)) * 2 + core)
        return jnp.stack(tiles).astype(jnp.int32)

    where = {
        "A": places(v, (0, 1)),
        "B": places(v, (2, 3)),
        "C": places(1 - v, (0, 1)),
        "D": places(1 - v, (2, 3)),
    }
    mine, peer = {}, {}
    parts = {}
    made = {}
    last, out = acts, None

    for step in ORDER:
        if step == "SA":
            mine["A"], last = stack(own, near, last)
            peer["A"] = swap(mine["A"], "c")
            mine["B"] = exchange(mine["A"], "x", 1)
            continue
        if step == "hV":
            other, last = hold(other, last)
            beyond = exchange(other, "x", 0)
            continue
        if step == "SC":
            mine["C"], last = stack(other, beyond, last)
            peer["C"] = swap(mine["C"], "c")
            mine["D"] = exchange(mine["C"], "x", 1)
            continue
        if step in ("hB", "hD"):
            name = step[1]
            mine[name], last = hold(mine[name], last)
            peer[name] = swap(mine[name], "c")
            continue
        name, stage = step[0], int(step[1])
        if stage == 7:
            out, last = place(out, *made[name], where[name], weights, last)
            continue
        if stage == 0:
            send, keep, last = fisher_parts(
                acts, mine[name], peer[name], weights, where[name], last
            )
            parts[name] = [(keep, 0)]
        elif stage < 4:
            rows, start = ((128, 0), (64, 128), (64, 192))[stage - 1]
            pairs = [(a, start - f) for a, f in parts[name]]
            send, last = add_up(pairs, rows, last, False)
        elif stage == 4:
            send, last = add_up(made[name], 64, last, True)
        else:
            send, last = join(made[name][0], made[name][1], last)
        axis, which = EXCHANGES[stage]
        came = exchange(send, axis, which)
        if stage == 0:
            parts[name].append((came, 0))
        elif stage < 3:
            parts[name].append((came, start + rows))
        elif stage == 3:
            made[name] = [(send, 0), (came, 0)]
        else:
            made[name] = [came, send]
    return out


def solution(mesh):
    fine = Mesh(mesh.devices.reshape(4, 4, 2, 4, 2), ("y", "w", "v", "x", "c"))
    mp, tp = ("y", "w"), ("v", "x", "c")
    in_specs = (P(mp, None, None, tp), P(mp, None, None, tp), P(mp, tp, None))
    return jax.shard_map(
        on_device, mesh=fine, in_specs=in_specs, out_specs=P(tp, None), check_vma=False
    )
```
